32 devices in a mesh: groups: 2 (over x), pool: 2 (over core), tensor: 8 (over z, y).
Axes of the slice: x: 2, y: 2, z: 4, core: 2. Of those that a mesh axis runs over, the one named last changes fastest.
Arguments:
- rows: bfloat16 [512, 8192], P(('groups', 'pool', 'tensor')), parts along dimension 0, may hold values from -6 to 6
- norm_gain: float32 [8192], replicated, may hold values from 0.1 to 1.9
- w_query: bfloat16 [8192, 8192], P(None, ('pool', 'tensor')), may hold values from -0.0625 to 0.0625
- w_keyval: bfloat16 [8192, 2048], P(None, ('pool', 'tensor')), may hold values from -0.125 to 0.125
- w_out: bfloat16 [8192, 8192], P(('pool', 'tensor')), may hold values from -0.25 to 0.25
- key_cache: bfloat16 [512, 256, 1024], P(('groups', 'pool', 'tensor')), parts along dimension 0, may hold values from -104 to 104
- value_cache: bfloat16 [512, 256, 1024], P(('groups', 'pool', 'tensor')), parts along dimension 0, may hold values from -6 to 6
- lengths: int32 [512], P('groups'), parts along dimension 0, may hold values from 1 to 256, as said below
- slot_of: int32 [512], P('groups'), parts along dimension 0, may hold values from 0 to 255, each once
Outputs:
- projected: bfloat16 [512, 8192], P(('groups', 'pool', 'tensor')), parts along dimension 0
The draws below stay inside these ranges and needn't reach their ends.
There are 2 independent parts, one for each index of `groups`. The reference program is written for one: setup_inputs(seed, part) draws one part's arguments, and reference() takes and returns one part's arrays. A program takes and returns all parts, laid end to end along the dimension named above; an argument that names none is the same for every part. Nothing has to cross between parts.
Inputs may be any that keep to these rules, and one draw needn't show every extreme that they name: `slot_of`: slots 16 * i to 16 * (i + 1) - 1 lie on index i of pool+tensor; every slot belongs to exactly one request. `lengths`: some request has exactly 256 cached tokens.
All inputs are finite; a program needn't handle non-finite values.
Results may differ from the reference program's by a relative error of at most 0.024.
Values may be sent and summed in bfloat16 or wider, within the bound.
A program may use at most 128 MiB of HBM per device.

```python
import jax
import jax.numpy as jnp
from jax import lax

D = 8192
HEADS = 64
KVH = 8
HD = 128
L = 256
REQUESTS = 256
N_POOL = 2
N_TENSOR = 8


def draw_lengths(key, part):
    key_top = jax.random.fold_in(key, 11)
    key_val = jax.random.fold_in(key, 12)
    key_pick = jax.random.fold_in(key, 13)
    upper = jax.random.randint(key_top, (REQUESTS,), 1, L + 1)
    raw = jax.random.randint(key_val, (REQUESTS,), 0, L)
    values = raw % upper + 1
    chosen = jax.random.randint(key_pick, (), 0, REQUESTS)
    return jnp.where(jnp.arange(REQUESTS) == chosen, L, values).astype(jnp.int32)


def draw_key_cache(key, part):
    base = jax.random.fold_in(key, 21)
    values = jnp.clip(2.0 * jax.random.normal(jax.random.fold_in(base, 5), (REQUESTS, L, KVH, HD), jnp.float32), -12.0, 12.0)
    return values.reshape(REQUESTS, L, KVH * HD).astype(jnp.bfloat16)


def shard_levels(key, dims, shards, low, high):
    loudness, own = 1.0, jax.random.fold_in(key, 6)
    for position, shards_of in shards:
        draws = jnp.exp(jax.random.uniform(jax.random.fold_in(own, position), (shards_of,), jnp.float32, low / len(shards), high / len(shards)))
        loudness = loudness * jnp.repeat(draws, dims[position] // shards_of).reshape([-1 if axis == position else 1 for axis in range(len(dims))])
    return loudness


def centred(own_key, dims, width, most, shards=(), held_as=jnp.bfloat16):
    entries = jax.random.normal(own_key, dims, jnp.float32) * width
    if len(shards) > 0:
        entries = shard_levels(own_key, dims, shards, -0.22, 0.18) * entries
    return jnp.clip(entries, min=-most, max=most).astype(held_as)


def setup_inputs(seed: int = 0, part: int = 0) -> dict:
    key_list = jax.random.split(jax.random.key(seed), 10)
    own_keys = jax.random.split(jax.random.fold_in(key_list[9], part), 10)
    rows = centred(own_keys[0], (REQUESTS, D), 1.0, 6.0, ((0, 16),))
    norm_gain = jnp.clip(1.0 + 0.18 * jax.random.normal(key_list[1], (D,), jnp.float32), 0.1, 1.9)
    w_query = centred(key_list[2], (D, HEADS * HD), D ** -0.5, 0.0625, ((1, 16),))
    w_keyval = centred(key_list[3], (D, 2 * KVH * HD), (D // 4) ** -0.5, 0.125, ((1, 16),))
    w_out = centred(key_list[4], (HEADS * HD, D), (HEADS * HD // 16) ** -0.5, 0.25, ((0, 16),))
    key_cache = draw_key_cache(jax.random.fold_in(jax.random.fold_in(key_list[9], part), 71), part)
    value_cache = centred(own_keys[6], (REQUESTS, L, KVH * HD), 1.0, 6.0, ((0, 16),))
    lengths = draw_lengths(jax.random.fold_in(jax.random.fold_in(key_list[9], part), 71), part)
    slot_of = jax.random.permutation(own_keys[8], REQUESTS).astype(jnp.int32)
    return dict(rows=rows, norm_gain=norm_gain, w_query=w_query, w_keyval=w_keyval, w_out=w_out, key_cache=key_cache, value_cache=value_cache, lengths=lengths, slot_of=slot_of)


EPS = 1e-05

def reference(rows, norm_gain, w_query, w_keyval, w_out, key_cache, value_cache, lengths, slot_of):
    values32 = rows.astype(jnp.float32)
    normed = (values32 * lax.rsqrt(lax.optimization_barrier(jnp.mean(values32 * values32, axis=1, keepdims=True)) + EPS) * norm_gain.astype(jnp.float32)).astype(jnp.bfloat16)
    queries = jnp.dot(normed, w_query, preferred_element_type=jnp.float32).astype(jnp.bfloat16)
    keyvals = jnp.dot(normed, w_keyval, preferred_element_type=jnp.float32).astype(jnp.bfloat16)
    group = HEADS // KVH
    positions = jnp.arange(L, dtype=jnp.int32)
    scale = HD ** (-0.5)

    def attend(inputs):
        query, keyval, slot, length = inputs
        cached_keys = lax.dynamic_index_in_dim(key_cache, slot, 0, keepdims=False).astype(jnp.float32).reshape(L, KVH, HD)
        cached_values = lax.dynamic_index_in_dim(value_cache, slot, 0, keepdims=False).astype(jnp.float32).reshape(L, KVH, HD)
        heads = query.astype(jnp.float32).reshape(KVH, group, HD)
        new_key = keyval[:KVH * HD].astype(jnp.float32).reshape(KVH, HD)
        new_value = keyval[KVH * HD:].astype(jnp.float32).reshape(KVH, HD)
        scores = jnp.einsum('kgd,lkd->kgl', heads, cached_keys) * scale
        scores = jnp.where((positions < length)[None, None, :], scores, -1e+30)
        own = jnp.einsum('kgd,kd->kg', heads, new_key) * scale
        top = jnp.maximum(lax.optimization_barrier(jnp.max(scores, axis=2)), own)
        probs = jnp.exp(scores - top[..., None])
        own_prob = jnp.exp(own - top)
        totals = lax.optimization_barrier(jnp.sum(probs, axis=2)) + own_prob
        probs_low = lax.optimization_barrier(probs.astype(jnp.bfloat16)).astype(jnp.float32)
        own_low = lax.optimization_barrier(own_prob.astype(jnp.bfloat16)).astype(jnp.float32)
        weighted = jnp.einsum('kgl,lkd->kgd', probs_low, cached_values) + own_low[..., None] * new_value[:, None, :]
        return (weighted / totals[..., None]).astype(jnp.bfloat16).reshape(HEADS * HD)
    attended = lax.map(attend, (queries, keyvals, slot_of.astype(jnp.int32), lengths.astype(jnp.int32)))
    pieces = N_POOL * N_TENSOR
    piece = HEADS * HD // pieces
    att_parts = attended.reshape(REQUESTS, pieces, piece)
    weight_parts = w_out.reshape(pieces, piece, D)

    def add_part(total, index):
        part_att = lax.dynamic_index_in_dim(att_parts, index, 1, keepdims=False)
        part_weight = lax.dynamic_index_in_dim(weight_parts, index, 0, keepdims=False)
        term = jnp.dot(part_att, part_weight, preferred_element_type=jnp.float32)
        term = lax.optimization_barrier(term.astype(jnp.bfloat16)).astype(jnp.float32)
        return (total + term, None)
    summed, _ = lax.scan(add_part, jnp.zeros((REQUESTS, D), jnp.float32), jnp.arange(pieces, dtype=jnp.int32))
    return summed.astype(jnp.bfloat16)
```

```python
import functools

import jax
import jax.numpy as jnp
from jax import lax
from jax.experimental import pallas as pl
from jax.experimental.pallas import tpu as pltpu
from jax.sharding import PartitionSpec as P

HD = 128
EPS = 1e-05
HALVES = 2
SUBS = 4
MESH = pl.DeviceIdType.MESH


def kernel(
    cfg,
    lens_ref, rows_ref, gain_ref, sort_ref, back_ref, wq_hbm, wkv_hbm, wo_hbm, k_hbm, v_hbm,
    out_ref,
    x_buf, wq, wkv, wo, kc, vc, acc_q, acc_kv, cols, sendq, arrived, qbuf, kbuf, vbuf, kvflat,
    obuf, sendo, returned, inr, pbuf, recvp, first, rbuf,
    load_sem, ag_send, ag_recv, core_send, core_recv, a_send, a_recv, b_send, b_recv,
    p_send, p_recv, r_send, r_recv,
):
    pools, ring, heads, kvh, rows_dev = cfg
    n = pools * ring
    group = heads // kvh
    slots_dev, length = kc.shape[0], kc.shape[1]
    depth = rows_ref.shape[1]
    query_cols = wq.shape[1]
    kv_cols = wkv.shape[1]
    scale = HD ** (-0.5)
    pool = lax.axis_index("pool")
    t_me = lax.axis_index("tensor")
    me = pool * ring + t_me
    half_ring = ring // 2

    def tensor_at(p):
        high = p // half_ring
        return (1 - high) * (2 * p) + high * (2 * (ring - 1 - p) + 1)

    odd = lax.rem(t_me, 2)
    pos = (1 - odd) * (t_me // 2) + odd * (ring - 1 - t_me // 2)

    def at(offset):
        return tensor_at(lax.rem(pos + offset + 2 * ring, ring))

    right = {"tensor": at(1)}
    left = {"tensor": at(-1)}
    other = {"pool": 1 - pool}

    loads = [
        pltpu.make_async_copy(src, dst, load_sem.at[i])
        for i, (src, dst) in enumerate(
            [(wq_hbm, wq), (wkv_hbm, wkv), (k_hbm, kc), (v_hbm, vc), (wo_hbm, wo)]
        )
    ]
    barrier = pltpu.get_barrier_semaphore()

    def greet(o, _):
        peer = lax.rem(me + o, n)
        pl.semaphore_signal(
            barrier, inc=1, device_id={"pool": peer // ring, "tensor": lax.rem(peer, ring)},
            device_id_type=MESH,
        )
        return 0

    lax.fori_loop(1, n, greet, 0)
    for load in loads:
        load.start()

    def rows_of(p, t):
        return pl.ds(pl.multiple_of((p * ring + t) * rows_dev, rows_dev), rows_dev)

    values = rows_ref[...].astype(jnp.float32)
    normed = values * lax.rsqrt(jnp.mean(values * values, axis=1, keepdims=True) + EPS)
    x_buf[rows_of(pool, t_me), :] = (normed * gain_ref[...]).astype(jnp.bfloat16)
    pl.semaphore_wait(barrier, n - 1)

    width = depth // HALVES

    def block(p, t, c):
        return x_buf.at[rows_of(p, t), pl.ds(c * width, width)]

    sent = []

    def ring_copy(way, dist, c):
        t = at(-dist) if way == 0 else at(dist)
        ref = block(pool, t, c)
        return pltpu.make_async_remote_copy(
            ref, ref, ag_send.at[way, dist - 1, c], ag_recv.at[way, dist - 1, c],
            device_id=right if way == 0 else left, device_id_type=MESH,
        )

    def ring_send(way, dist, c):
        t = at(-(dist - 1)) if way == 0 else at(dist - 1)
        ref = block(pool, t, c)
        copy = pltpu.make_async_remote_copy(
            ref, ref, ag_send.at[way, dist - 1, c], ag_recv.at[way, dist - 1, c],
            device_id=right if way == 0 else left, device_id_type=MESH,
        )
        copy.start()
        sent.append(copy)

    def core_copy(p, k, c):
        ref = block(p, at(k), c)
        return pltpu.make_async_remote_copy(
            ref, ref, core_send.at[k, c], core_recv.at[k, c], device_id=other, device_id_type=MESH,
        )

    def core_send_start(k, c):
        copy = core_copy(pool, k % ring, c)
        copy.start()
        sent.append(copy)

    def travels(way, dist, c):
        return dist < half_ring or (dist == half_ring and c == way)

    for c in range(HALVES):
        for way in range(2):
            cc = c if way == 0 else HALVES - 1 - c
            if travels(way, 1, cc):
                ring_send(way, 1, cc)
    for c in range(HALVES):
        core_send_start(0, c)
    for dist in range(1, half_ring + 1):
        for c in range(HALVES):
            for way in range(2):
                cc = c if way == 0 else HALVES - 1 - c
                if travels(way, dist, cc):
                    ring_copy(way, dist, cc).wait_recv()
                    if travels(way, dist + 1, cc):
                        ring_send(way, dist + 1, cc)
                    core_send_start(-dist if way == 0 else dist, cc)
    for k in range(ring):
        for c in range(HALVES):
            core_copy(1 - pool, k, c).wait_recv()
    for copy in sent:
        copy.wait_send()

    loads[0].wait()
    loads[1].wait()

    acc_q[...] = jnp.zeros_like(acc_q)
    acc_kv[...] = jnp.zeros_like(acc_kv)
    step = depth // 8

    def project(i, _):
        ks = pl.ds(pl.multiple_of(i * step, step), step)
        acc_q[...] += jnp.dot(x_buf[:, ks], wq[ks, :], preferred_element_type=jnp.float32)
        acc_kv[...] += jnp.dot(x_buf[:, ks], wkv[ks, :], preferred_element_type=jnp.float32)
        return 0

    lax.fori_loop(0, 8, project, 0)
    cols[:, :query_cols] = acc_q[...].astype(jnp.bfloat16)
    cols[:, query_cols:] = acc_kv[...].astype(jnp.bfloat16)
    in_slots = jnp.dot(sort_ref[...], cols[...], preferred_element_type=jnp.float32).astype(jnp.bfloat16)
    sendq[...] = in_slots.reshape(sendq.shape)

    def exchange(src, dst, s_sem, r_sem):
        def copy_to(peer, slot):
            return pltpu.make_async_remote_copy(
                src.at[peer], dst.at[slot], s_sem.at[peer], r_sem.at[slot],
                device_id={"pool": peer // ring, "tensor": lax.rem(peer, ring)},
                device_id_type=MESH,
            )

        def start(o, _):
            copy_to(lax.rem(me + o, n), me).start()
            return 0

        def finish(o, _):
            peer = lax.rem(me + o, n)
            copy_to(peer, peer).wait()
            return 0

        lax.fori_loop(1, n, start, 0)
        dst[me] = src[me]
        lax.fori_loop(1, n, finish, 0)

    exchange(sendq, arrived, a_send, a_recv)

    hp = query_cols // HD
    for i in range(n):
        for j in range(hp):
            qbuf[:, i * hp + j, :] = arrived[i, :, j * HD:(j + 1) * HD].astype(jnp.float32)
        kvflat[:, i * kv_cols:(i + 1) * kv_cols] = arrived[i, :, query_cols:].astype(jnp.float32)
    for k in range(kvh):
        kbuf[:, k, :] = kvflat[:, k * HD:(k + 1) * HD]
        vbuf[:, k, :] = kvflat[:, (kvh + k) * HD:(kvh + k + 1) * HD]
    loads[2].wait()
    loads[3].wait()

    row_head = lax.broadcasted_iota(jnp.int32, (heads, kvh * HD), 0) // group
    col_head = lax.broadcasted_iota(jnp.int32, (heads, kvh * HD), 1) // HD
    diagonal = row_head == col_head

    def attend(s):
        q = qbuf[s]
        wide = jnp.where(diagonal, jnp.concatenate([q] * kvh, axis=1), 0.0).astype(jnp.bfloat16)
        scores = lax.dot_general(
            wide, kc[s], (((1,), (1,)), ((), ())), preferred_element_type=jnp.float32
        ) * scale
        live = lax.broadcasted_iota(jnp.int32, (heads, length), 1) < lens_ref[s]
        scores = jnp.where(live, scores, -1e30)
        nk = jnp.broadcast_to(kbuf[s][:, None, :], (kvh, group, HD)).reshape(heads, HD)
        nv = jnp.broadcast_to(vbuf[s][:, None, :], (kvh, group, HD)).reshape(heads, HD)
        own = jnp.sum(q * nk, axis=1, keepdims=True) * scale
        top = jnp.maximum(jnp.max(scores, axis=1, keepdims=True), own)
        probs = jnp.exp(scores - top)
        own_prob = jnp.exp(own - top)
        totals = jnp.sum(probs, axis=1, keepdims=True) + own_prob
        full = jnp.dot(probs.astype(jnp.bfloat16), vc[s], preferred_element_type=jnp.float32)
        mine = jnp.concatenate(
            [full[k * group:(k + 1) * group, k * HD:(k + 1) * HD] for k in range(kvh)], axis=0
        )
        mine = mine + own_prob.astype(jnp.bfloat16).astype(jnp.float32) * nv
        obuf[s] = mine / totals

    def attend_pair(i, _):
        attend(2 * i)
        attend(2 * i + 1)
        return 0

    lax.fori_loop(0, slots_dev // 2, attend_pair, 0)

    for i in range(n):
        for j in range(hp):
            sendo[i, :, j * HD:(j + 1) * HD] = obuf[:, i * hp + j, :].astype(jnp.bfloat16)
    exchange(sendo, returned, b_send, b_recv)

    requests = n * rows_dev
    inr[...] = jnp.dot(
        back_ref[...], returned[...].reshape(requests, query_cols), preferred_element_type=jnp.float32
    ).astype(jnp.bfloat16)
    loads[4].wait()

    tiles = 2 * SUBS
    tile = depth // tiles
    half_rows = ring * rows_dev

    def pair_copy(c):
        return pltpu.make_async_remote_copy(
            pbuf.at[c, pl.ds(pl.multiple_of((1 - pool) * half_rows, half_rows), half_rows)],
            recvp.at[c], p_send.at[c], p_recv.at[c], device_id=other, device_id_type=MESH,
        )

    for sub in range(SUBS):
        for way in range(2):
            c = way * SUBS + sub
            pbuf[c] = jnp.dot(
                inr[...], wo[:, c * tile:(c + 1) * tile], preferred_element_type=jnp.float32
            ).astype(jnp.bfloat16)
            pair_copy(c).start()

    def pair_sum(c, t):
        mine = pbuf[c, rows_of(pool, t), :].astype(jnp.float32)
        theirs = recvp[c, pl.ds(pl.multiple_of(t * rows_dev, rows_dev), rows_dev), :]
        return mine + theirs.astype(jnp.float32)

    def hop_copy(src, way, hop, sub):
        return pltpu.make_async_remote_copy(
            src, rbuf.at[way, hop, sub], r_send.at[way, hop, sub], r_recv.at[way, hop, sub],
            device_id=right if way == 0 else left, device_id_type=MESH,
        )

    for sub in range(SUBS):
        for way in range(2):
            c = way * SUBS + sub
            pair_copy(c).wait_recv()
            t = at(-1) if way == 0 else at(1)
            first[way, sub] = pair_sum(c, t).astype(jnp.bfloat16)
            hop_copy(first.at[way, sub], way, 0, sub).start()

    def hop_step(hop, _):
        for sub in range(SUBS):
            for way in range(2):
                c = way * SUBS + sub
                here = rbuf.at[way, hop, sub]
                hop_copy(here, way, hop, sub).wait_recv()
                t = at(-2 - hop) if way == 0 else at(2 + hop)
                rbuf[way, hop, sub] = (
                    rbuf[way, hop, sub].astype(jnp.float32) + pair_sum(c, t)
                ).astype(jnp.bfloat16)
                hop_copy(here, way, hop + 1, sub).start()
        return 0

    lax.fori_loop(0, ring - 2, hop_step, 0)
    last = ring - 2
    for sub in range(SUBS):
        for way in range(2):
            c = way * SUBS + sub
            hop_copy(rbuf.at[way, last, sub], way, last, sub).wait_recv()
            out_ref[:, c * tile:(c + 1) * tile] = (
                rbuf[way, last, sub].astype(jnp.float32) + pair_sum(c, t_me)
            ).astype(out_ref.dtype)

    for sub in range(SUBS):
        for way in range(2):
            pair_copy(way * SUBS + sub).wait_send()
            hop_copy(first.at[way, sub], way, 0, sub).wait_send()

    def drain(hop, _):
        for sub in range(SUBS):
            for way in range(2):
                hop_copy(rbuf.at[way, hop - 1, sub], way, hop, sub).wait_send()
        return 0

    lax.fori_loop(1, ring - 1, drain, 0)


def body(rows, norm_gain, w_query, w_keyval, w_out, key_cache, value_cache, lengths, slot_of):
    pools, ring = lax.axis_size("pool"), lax.axis_size("tensor")
    n = pools * ring
    rows_dev, depth = rows.shape
    slots_dev, length, kv_width = key_cache.shape
    kvh = kv_width // HD
    query_cols, kv_cols = w_query.shape[1], w_keyval.shape[1]
    heads = query_cols * n // HD
    width = query_cols + kv_cols
    requests = rows_dev * n
    half_ring = ring // 2
    tile = depth // (2 * SUBS)
    slot_ids = jnp.arange(requests, dtype=jnp.int32)
    sort_map = (slot_of[None, :] == slot_ids[:, None]).astype(jnp.bfloat16)
    back_map = (slot_of[:, None] == slot_ids[None, :]).astype(jnp.bfloat16)
    own_slots = lax.axis_index(("pool", "tensor")) * slots_dev + jnp.arange(slots_dev, dtype=jnp.int32)
    slot_len = jnp.sum(jnp.where(slot_of[None, :] == own_slots[:, None], lengths[None, :], 0), axis=1)
    bf16, f32 = jnp.bfloat16, jnp.float32
    vmem = pl.BlockSpec(memory_space=pltpu.VMEM)
    hbm = pl.BlockSpec(memory_space=pl.ANY)
    dma = pltpu.SemaphoreType.DMA
    return pl.pallas_call(
        functools.partial(kernel, (pools, ring, heads, kvh, rows_dev)),
        out_shape=jax.ShapeDtypeStruct((rows_dev, depth), bf16),
        in_specs=[pl.BlockSpec(memory_space=pltpu.SMEM)] + [vmem] * 4 + [hbm] * 5,
        out_specs=vmem,
        scratch_shapes=[
            pltpu.VMEM((requests, depth), bf16),
            pltpu.VMEM(w_query.shape, bf16),
            pltpu.VMEM(w_keyval.shape, bf16),
            pltpu.VMEM(w_out.shape, bf16),
            pltpu.VMEM(key_cache.shape, bf16),
            pltpu.VMEM(value_cache.shape, bf16),
            pltpu.VMEM((requests, query_cols), f32),
            pltpu.VMEM((requests, kv_cols), f32),
            pltpu.VMEM((requests, width), bf16),
            pltpu.VMEM((n, slots_dev, width), bf16),
            pltpu.VMEM((n, slots_dev, width), bf16),
            pltpu.VMEM((slots_dev, heads, HD), f32),
            pltpu.VMEM((slots_dev, kvh, HD), f32),
            pltpu.VMEM((slots_dev, kvh, HD), f32),
            pltpu.VMEM((slots_dev, 2 * kvh * HD), f32),
            pltpu.VMEM((slots_dev, heads, HD), f32),
            pltpu.VMEM((n, slots_dev, query_cols), bf16),
            pltpu.VMEM((n, slots_dev, query_cols), bf16),
            pltpu.VMEM((requests, query_cols), bf16),
            pltpu.VMEM((2 * SUBS, requests, tile), bf16),
            pltpu.VMEM((2 * SUBS, requests // pools, tile), bf16),
            pltpu.VMEM((2, SUBS, rows_dev, tile), bf16),
            pltpu.VMEM((2, ring - 1, SUBS, rows_dev, tile), bf16),
            dma((5,)),
            dma((2, half_ring, HALVES)),
            dma((2, half_ring, HALVES)),
            dma((ring, HALVES)),
            dma((ring, HALVES)),
            dma((n,)),
            dma((n,)),
            dma((n,)),
            dma((n,)),
            dma((2 * SUBS,)),
            dma((2 * SUBS,)),
            dma((2, ring - 1, SUBS)),
            dma((2, ring - 1, SUBS)),
        ],
        compiler_params=pltpu.CompilerParams(
            collective_id=0, has_side_effects=True, vmem_limit_bytes=60 * 2**20
        ),
        name="decode_step",
    )(
        slot_len, rows, norm_gain.reshape(1, depth), sort_map, back_map,
        w_query, w_keyval, w_out, key_cache, value_cache,
    )


def solution(mesh):
    placed = (
        P(("groups", "pool", "tensor"), None),
        P(),
        P(None, ("pool", "tensor")),
        P(None, ("pool", "tensor")),
        P(("pool", "tensor"), None),
        P(("groups", "pool", "tensor"), None, None),
        P(("groups", "pool", "tensor"), None, None),
        P("groups"),
        P("groups"),
    )
    return jax.shard_map(
        body,
        mesh=mesh,
        in_specs=placed,
        out_specs=P(("groups", "pool", "tensor"), None),
        check_vma=False,
    )
```

```python
import functools

import jax
import jax.numpy as jnp
from jax import lax
from jax.experimental import pallas as pl
from jax.experimental.pallas import tpu as pltpu
from jax.sharding import PartitionSpec as P

HD = 128
EPS = 1e-05
CHUNKS = 4
SUBS = 4
TOGETHER = 4
MESH = pl.DeviceIdType.MESH


def kernel(
    cfg,
    slots_ref, lens_ref, rows_ref, gain_ref, wq_hbm, wkv_hbm, wo_hbm, k_hbm, v_hbm,
    out_ref,
    x_buf, wq, wkv, wo, kc, vc, acc_q, acc_kv, cols, sendq, arrived, qbuf, kbuf, vbuf, kvflat,
    obuf, sendo, returned, sort_map, lens, inr, pbuf, recvp, first, rbuf,
    load_sem, ag_send, ag_recv, core_send, core_recv, a_send, a_recv, b_send, b_recv,
    p_send, p_recv, r_send, r_recv,
):
    pools, ring, heads, kvh, rows_dev = cfg
    n = pools * ring
    group = heads // kvh
    slots_dev, length = kc.shape[0], kc.shape[1]
    depth = rows_ref.shape[1]
    query_cols = wq.shape[1]
    kv_cols = wkv.shape[1]
    scale = HD ** (-0.5)
    pool = lax.axis_index("pool")
    t_me = lax.axis_index("tensor")
    me = pool * ring + t_me
    half_ring = ring // 2

    def tensor_at(p):
        high = p // half_ring
        return (1 - high) * (2 * p) + high * (2 * (ring - 1 - p) + 1)

    odd = lax.rem(t_me, 2)
    pos = (1 - odd) * (t_me // 2) + odd * (ring - 1 - t_me // 2)

    def at(offset):
        return tensor_at(lax.rem(pos + offset + 2 * ring, ring))

    right = {"tensor": at(1)}
    left = {"tensor": at(-1)}
    other = {"pool": 1 - pool}

    loads = [
        pltpu.make_async_copy(src, dst, load_sem.at[i])
        for i, (src, dst) in enumerate(
            [(wq_hbm, wq), (wkv_hbm, wkv), (k_hbm, kc), (v_hbm, vc), (wo_hbm, wo)]
        )
    ]
    barrier = pltpu.get_barrier_semaphore()

    def greet(o, _):
        peer = lax.rem(me + o, n)
        pl.semaphore_signal(
            barrier, inc=1, device_id={"pool": peer // ring, "tensor": lax.rem(peer, ring)},
            device_id_type=MESH,
        )
        return 0

    lax.fori_loop(1, n, greet, 0)

    def rows_of(p, t):
        return pl.ds(pl.multiple_of((p * ring + t) * rows_dev, rows_dev), rows_dev)

    values = rows_ref[...].astype(jnp.float32)
    normed = values * lax.rsqrt(jnp.mean(values * values, axis=1, keepdims=True) + EPS)
    x_buf[rows_of(pool, t_me), :] = (normed * gain_ref[...]).astype(jnp.bfloat16)
    pl.semaphore_wait(barrier, n - 1)

    width = depth // CHUNKS

    def block(p, t, c):
        return x_buf.at[rows_of(p, t), pl.ds(c * width, width)]

    sent = []

    def ring_copy(way, dist, c):
        t = at(-dist) if way == 0 else at(dist)
        ref = block(pool, t, c)
        return pltpu.make_async_remote_copy(
            ref, ref, ag_send.at[way, dist - 1, c], ag_recv.at[way, dist - 1, c],
            device_id=right if way == 0 else left, device_id_type=MESH,
        )

    def ring_send(way, dist, c):
        t = at(-(dist - 1)) if way == 0 else at(dist - 1)
        ref = block(pool, t, c)
        copy = pltpu.make_async_remote_copy(
            ref, ref, ag_send.at[way, dist - 1, c], ag_recv.at[way, dist - 1, c],
            device_id=right if way == 0 else left, device_id_type=MESH,
        )
        copy.start()
        sent.append(copy)

    def core_copy(p, k, c):
        ref = block(p, at(k), c)
        return pltpu.make_async_remote_copy(
            ref, ref, core_send.at[k, c], core_recv.at[k, c], device_id=other, device_id_type=MESH,
        )

    def core_send_start(k, c):
        copy = core_copy(pool, k % ring, c)
        copy.start()
        sent.append(copy)

    def travels(way, dist, c):
        return dist < half_ring or (dist == half_ring and c * 2 // CHUNKS == way)

    for c in range(CHUNKS):
        for way in range(2):
            cc = c if way == 0 else CHUNKS - 1 - c
            if travels(way, 1, cc):
                ring_send(way, 1, cc)
    for c in range(CHUNKS):
        core_send_start(0, c)
    loads[0].start()
    loads[1].start()

    requests = n * rows_dev
    slot_row = slots_ref[...]
    sort_map[...] = jnp.where(
        lax.broadcasted_iota(jnp.int32, (requests, requests), 0) == slot_row, 1.0, 0.0
    ).astype(jnp.bfloat16)
    own_slots = lax.broadcasted_iota(jnp.int32, (slots_dev, requests), 0) + me * slots_dev
    own_len = jnp.sum(
        jnp.where(own_slots == slot_row, lens_ref[...].astype(jnp.float32), 0.0), axis=1, keepdims=True
    )
    lens[...] = jnp.broadcast_to(own_len, lens.shape)

    for dist in range(1, half_ring + 1):
        for c in range(CHUNKS):
            for way in range(2):
                cc = c if way == 0 else CHUNKS - 1 - c
                if travels(way, dist, cc):
                    ring_copy(way, dist, cc).wait_recv()
                    if travels(way, dist + 1, cc):
                        ring_send(way, dist + 1, cc)
                    core_send_start(-dist if way == 0 else dist, cc)
        if dist <= 2:
            loads[1 + dist].start()
    for k in range(ring):
        for c in range(CHUNKS):
            core_copy(1 - pool, k, c).wait_recv()

    loads[0].wait()
    loads[1].wait()

    acc_q[...] = jnp.zeros_like(acc_q)
    acc_kv[...] = jnp.zeros_like(acc_kv)
    step = depth // 8

    def project(i, _):
        ks = pl.ds(pl.multiple_of(i * step, step), step)
        acc_q[...] += jnp.dot(x_buf[:, ks], wq[ks, :], preferred_element_type=jnp.float32)
        acc_kv[...] += jnp.dot(x_buf[:, ks], wkv[ks, :], preferred_element_type=jnp.float32)
        return 0

    lax.fori_loop(0, 8, project, 0)
    cols[:, :query_cols] = acc_q[...].astype(jnp.bfloat16)
    cols[:, query_cols:] = acc_kv[...].astype(jnp.bfloat16)
    in_slots = jnp.dot(sort_map[...], cols[...], preferred_element_type=jnp.float32).astype(jnp.bfloat16)
    sendq[...] = in_slots.reshape(sendq.shape)

    def exchange(src, dst, s_sem, r_sem):
        def copy_to(peer, slot):
            return pltpu.make_async_remote_copy(
                src.at[peer], dst.at[slot], s_sem.at[peer], r_sem.at[slot],
                device_id={"pool": peer // ring, "tensor": lax.rem(peer, ring)},
                device_id_type=MESH,
            )

        def start(o, _):
            copy_to(lax.rem(me + o, n), me).start()
            return 0

        def finish(o, _):
            peer = lax.rem(me + o, n)
            copy_to(peer, peer).wait()
            return 0

        lax.fori_loop(1, n, start, 0)
        dst[me] = src[me]
        lax.fori_loop(1, n, finish, 0)

    loads[4].start()
    exchange(sendq, arrived, a_send, a_recv)

    hp = query_cols // HD
    for i in range(n):
        for j in range(hp):
            qbuf[:, i * hp + j, :] = arrived[i, :, j * HD:(j + 1) * HD].astype(jnp.float32)
        kvflat[:, i * kv_cols:(i + 1) * kv_cols] = arrived[i, :, query_cols:].astype(jnp.float32)
    for k in range(kvh):
        kbuf[:, k, :] = kvflat[:, k * HD:(k + 1) * HD]
        vbuf[:, k, :] = kvflat[:, (kvh + k) * HD:(kvh + k + 1) * HD]
    loads[2].wait()
    loads[3].wait()

    row_head = lax.broadcasted_iota(jnp.int32, (heads, kvh * HD), 0) // group
    place = lax.broadcasted_iota(jnp.int32, (heads, length), 1).astype(jnp.float32)
    col_head = lax.broadcasted_iota(jnp.int32, (heads, kvh * HD), 1) // HD
    diagonal = row_head == col_head

    def attend(s):
        q = qbuf[s]
        wide = jnp.where(diagonal, jnp.concatenate([q] * kvh, axis=1), 0.0).astype(jnp.bfloat16)
        scores = lax.dot_general(
            wide, kc[s], (((1,), (1,)), ((), ())), preferred_element_type=jnp.float32
        ) * scale
        scores = jnp.where(place < lens[pl.ds(s, 1), :], scores, -1e30)
        nk = jnp.broadcast_to(kbuf[s][:, None, :], (kvh, group, HD)).reshape(heads, HD)
        nv = jnp.broadcast_to(vbuf[s][:, None, :], (kvh, group, HD)).reshape(heads, HD)
        own = jnp.sum(q * nk, axis=1, keepdims=True) * scale
        top = jnp.maximum(jnp.max(scores, axis=1, keepdims=True), own)
        probs = jnp.exp(scores - top)
        own_prob = jnp.exp(own - top)
        totals = jnp.sum(probs, axis=1, keepdims=True) + own_prob
        full = jnp.dot(probs.astype(jnp.bfloat16), vc[s], preferred_element_type=jnp.float32)
        mine = jnp.concatenate(
            [full[k * group:(k + 1) * group, k * HD:(k + 1) * HD] for k in range(kvh)], axis=0
        )
        mine = mine + own_prob.astype(jnp.bfloat16).astype(jnp.float32) * nv
        obuf[s] = mine / totals

    def attend_some(i, _):
        for j in range(TOGETHER):
            attend(TOGETHER * i + j)
        return 0

    lax.fori_loop(0, slots_dev // TOGETHER, attend_some, 0)

    for i in range(n):
        for j in range(hp):
            sendo[i, :, j * HD:(j + 1) * HD] = obuf[:, i * hp + j, :].astype(jnp.bfloat16)
    exchange(sendo, returned, b_send, b_recv)

    inr[...] = lax.dot_general(
        sort_map[...], returned[...].reshape(requests, query_cols), (((0,), (0,)), ((), ())),
        preferred_element_type=jnp.float32,
    ).astype(jnp.bfloat16)
    loads[4].wait()

    tiles = 2 * SUBS
    tile = depth // tiles
    half_rows = ring * rows_dev

    def pair_copy(c):
        return pltpu.make_async_remote_copy(
            pbuf.at[c, pl.ds(pl.multiple_of((1 - pool) * half_rows, half_rows), half_rows)],
            recvp.at[c], p_send.at[c], p_recv.at[c], device_id=other, device_id_type=MESH,
        )

    def pair_sum(c, t):
        mine = pbuf[c, rows_of(pool, t), :].astype(jnp.float32)
        theirs = recvp[c, pl.ds(pl.multiple_of(t * rows_dev, rows_dev), rows_dev), :]
        return mine + theirs.astype(jnp.float32)

    def hop_copy(src, way, hop, sub):
        return pltpu.make_async_remote_copy(
            src, rbuf.at[way, hop, sub], r_send.at[way, hop, sub], r_recv.at[way, hop, sub],
            device_id=right if way == 0 else left, device_id_type=MESH,
        )

    def set_off(sub):
        for way in range(2):
            c = way * SUBS + sub
            pair_copy(c).wait_recv()
            t = at(-1) if way == 0 else at(1)
            first[way, sub] = pair_sum(c, t).astype(jnp.bfloat16)
            hop_copy(first.at[way, sub], way, 0, sub).start()

    for sub in range(SUBS):
        for way in range(2):
            c = way * SUBS + sub
            pbuf[c] = jnp.dot(
                inr[...], wo[:, c * tile:(c + 1) * tile], preferred_element_type=jnp.float32
            ).astype(jnp.bfloat16)
            pair_copy(c).start()
        if sub >= 1:
            set_off(sub - 1)
    set_off(SUBS - 1)

    def hop_step(hop, _):
        for sub in range(SUBS):
            for way in range(2):
                c = way * SUBS + sub
                here = rbuf.at[way, hop, sub]
                hop_copy(here, way, hop, sub).wait_recv()
                t = at(-2 - hop) if way == 0 else at(2 + hop)
                rbuf[way, hop, sub] = (
                    rbuf[way, hop, sub].astype(jnp.float32) + pair_sum(c, t)
                ).astype(jnp.bfloat16)
                hop_copy(here, way, hop + 1, sub).start()
        return 0

    lax.fori_loop(0, ring - 2, hop_step, 0)
    last = ring - 2
    for sub in range(SUBS):
        for way in range(2):
            c = way * SUBS + sub
            hop_copy(rbuf.at[way, last, sub], way, last, sub).wait_recv()
            out_ref[:, c * tile:(c + 1) * tile] = (
                rbuf[way, last, sub].astype(jnp.float32) + pair_sum(c, t_me)
            ).astype(out_ref.dtype)

    for sub in range(SUBS):
        for way in range(2):
            pair_copy(way * SUBS + sub).wait_send()
            hop_copy(first.at[way, sub], way, 0, sub).wait_send()

    def drain(hop, _):
        for sub in range(SUBS):
            for way in range(2):
                hop_copy(rbuf.at[way, hop - 1, sub], way, hop, sub).wait_send()
        return 0

    lax.fori_loop(1, ring - 1, drain, 0)
    for copy in sent:
        copy.wait_send()


def body(rows, norm_gain, w_query, w_keyval, w_out, key_cache, value_cache, lengths, slot_of):
    pools, ring = lax.axis_size("pool"), lax.axis_size("tensor")
    n = pools * ring
    rows_dev, depth = rows.shape
    slots_dev, length, kv_width = key_cache.shape
    kvh = kv_width // HD
    query_cols, kv_cols = w_query.shape[1], w_keyval.shape[1]
    heads = query_cols * n // HD
    width = query_cols + kv_cols
    requests = rows_dev * n
    half_ring = ring // 2
    tile = depth // (2 * SUBS)
    bf16, f32 = jnp.bfloat16, jnp.float32
    vmem = pl.BlockSpec(memory_space=pltpu.VMEM)
    hbm = pl.BlockSpec(memory_space=pl.ANY)
    dma = pltpu.SemaphoreType.DMA
    return pl.pallas_call(
        functools.partial(kernel, (pools, ring, heads, kvh, rows_dev)),
        out_shape=jax.ShapeDtypeStruct((rows_dev, depth), bf16),
        in_specs=[vmem] * 4 + [hbm] * 5,
        out_specs=vmem,
        scratch_shapes=[
            pltpu.VMEM((requests, depth), bf16),
            pltpu.VMEM(w_query.shape, bf16),
            pltpu.VMEM(w_keyval.shape, bf16),
            pltpu.VMEM(w_out.shape, bf16),
            pltpu.VMEM(key_cache.shape, bf16),
            pltpu.VMEM(value_cache.shape, bf16),
            pltpu.VMEM((requests, query_cols), f32),
            pltpu.VMEM((requests, kv_cols), f32),
            pltpu.VMEM((requests, width), bf16),
            pltpu.VMEM((n, slots_dev, width), bf16),
            pltpu.VMEM((n, slots_dev, width), bf16),
            pltpu.VMEM((slots_dev, heads, HD), f32),
            pltpu.VMEM((slots_dev, kvh, HD), f32),
            pltpu.VMEM((slots_dev, kvh, HD), f32),
            pltpu.VMEM((slots_dev, 2 * kvh * HD), f32),
            pltpu.VMEM((slots_dev, heads, HD), f32),
            pltpu.VMEM((n, slots_dev, query_cols), bf16),
            pltpu.VMEM((n, slots_dev, query_cols), bf16),
            pltpu.VMEM((requests, requests), bf16),
            pltpu.VMEM((slots_dev, length), f32),
            pltpu.VMEM((requests, query_cols), bf16),
            pltpu.VMEM((2 * SUBS, requests, tile), bf16),
            pltpu.VMEM((2 * SUBS, requests // pools, tile), bf16),
            pltpu.VMEM((2, SUBS, rows_dev, tile), bf16),
            pltpu.VMEM((2, ring - 1, SUBS, rows_dev, tile), bf16),
            dma((5,)),
            dma((2, half_ring, CHUNKS)),
            dma((2, half_ring, CHUNKS)),
            dma((ring, CHUNKS)),
            dma((ring, CHUNKS)),
            dma((n,)),
            dma((n,)),
            dma((n,)),
            dma((n,)),
            dma((2 * SUBS,)),
            dma((2 * SUBS,)),
            dma((2, ring - 1, SUBS)),
            dma((2, ring - 1, SUBS)),
        ],
        compiler_params=pltpu.CompilerParams(
            collective_id=0, has_side_effects=True, vmem_limit_bytes=60 * 2**20
        ),
        name="decode_step",
    )(
        slot_of.reshape(1, requests), lengths.reshape(1, requests), rows, norm_gain.reshape(1, depth),
        w_query, w_keyval, w_out, key_cache, value_cache,
    )


def solution(mesh):
    placed = (
        P(("groups", "pool", "tensor"), None),
        P(),
        P(None, ("pool", "tensor")),
        P(None, ("pool", "tensor")),
        P(("pool", "tensor"), None),
        P(("groups", "pool", "tensor"), None, None),
        P(("groups", "pool", "tensor"), None, None),
        P("groups"),
        P("groups"),
    )
    return jax.shard_map(
        body,
        mesh=mesh,
        in_specs=placed,
        out_specs=P(("groups", "pool", "tensor"), None),
        check_vma=False,
    )
```

```python
import functools

import jax
import jax.numpy as jnp
from jax import lax
from jax.experimental import pallas as pl
from jax.experimental.pallas import tpu as pltpu
from jax.sharding import PartitionSpec as P

HD = 128
EPS = 1e-05
CHUNKS = 2
SUBS = 4
TOGETHER = 4
MESH = pl.DeviceIdType.MESH


def kernel(
    cfg,
    slots_ref, lens_ref, rows_ref, gain_ref, wq_hbm, wkv_hbm, wo_hbm, k_hbm, v_hbm,
    out_ref,
    x_buf, wq, wkv, wo, kc, vc, acc_q, acc_kv, cols, sendq, arrived, qbuf, kbuf, vbuf, kvflat,
    obuf, sendo, returned, sort_map, lens, inr, pbuf, recvp, first, rbuf,
    load_sem, ag_send, ag_recv, core_send, core_recv, a_send, a_recv, b_send, b_recv,
    p_send, p_recv, r_send, r_recv,
):
    pools, ring, heads, kvh, rows_dev = cfg
    n = pools * ring
    group = heads // kvh
    slots_dev, length = kc.shape[0], kc.shape[1]
    depth = rows_ref.shape[1]
    query_cols = wq.shape[1]
    kv_cols = wkv.shape[1]
    scale = HD ** (-0.5)
    pool = lax.axis_index("pool")
    t_me = lax.axis_index("tensor")
    me = pool * ring + t_me
    half_ring = ring // 2

    def tensor_at(p):
        high = p // half_ring
        return (1 - high) * (2 * p) + high * (2 * (ring - 1 - p) + 1)

    odd = lax.rem(t_me, 2)
    pos = (1 - odd) * (t_me // 2) + odd * (ring - 1 - t_me // 2)

    def at(offset):
        return tensor_at(lax.rem(pos + offset + 2 * ring, ring))

    right = {"tensor": at(1)}
    left = {"tensor": at(-1)}
    other = {"pool": 1 - pool}

    loads = [
        pltpu.make_async_copy(src, dst, load_sem.at[i])
        for i, (src, dst) in enumerate(
            [(wq_hbm, wq), (wkv_hbm, wkv), (k_hbm, kc), (v_hbm, vc), (wo_hbm, wo)]
        )
    ]
    barrier = pltpu.get_barrier_semaphore()

    for peer in (left, right, other):
        pl.semaphore_signal(barrier, inc=1, device_id=peer, device_id_type=MESH)

    def rows_of(p, t):
        return pl.ds(pl.multiple_of((p * ring + t) * rows_dev, rows_dev), rows_dev)

    values = rows_ref[...].astype(jnp.float32)
    normed = values * lax.rsqrt(jnp.mean(values * values, axis=1, keepdims=True) + EPS)
    x_buf[rows_of(pool, t_me), :] = (normed * gain_ref[...]).astype(jnp.bfloat16)
    pl.semaphore_wait(barrier, 3)

    width = depth // CHUNKS

    def block(p, t, c):
        return x_buf.at[rows_of(p, t), pl.ds(c * width, width)]

    sent = []

    def ring_copy(way, dist, c):
        t = at(-dist) if way == 0 else at(dist)
        ref = block(pool, t, c)
        return pltpu.make_async_remote_copy(
            ref, ref, ag_send.at[way, dist - 1, c], ag_recv.at[way, dist - 1, c],
            device_id=right if way == 0 else left, device_id_type=MESH,
        )

    def ring_send(way, dist, c):
        t = at(-(dist - 1)) if way == 0 else at(dist - 1)
        ref = block(pool, t, c)
        copy = pltpu.make_async_remote_copy(
            ref, ref, ag_send.at[way, dist - 1, c], ag_recv.at[way, dist - 1, c],
            device_id=right if way == 0 else left, device_id_type=MESH,
        )
        copy.start()
        sent.append(copy)

    def core_copy(p, k, c):
        ref = block(p, at(k), c)
        return pltpu.make_async_remote_copy(
            ref, ref, core_send.at[k, c], core_recv.at[k, c], device_id=other, device_id_type=MESH,
        )

    def core_send_start(k, c):
        copy = core_copy(pool, k % ring, c)
        copy.start()
        sent.append(copy)

    def travels(way, dist, c):
        return dist < half_ring or (dist == half_ring and c * 2 // CHUNKS == way)

    for c in range(CHUNKS):
        for way in range(2):
            cc = c if way == 0 else CHUNKS - 1 - c
            if travels(way, 1, cc):
                ring_send(way, 1, cc)
    for c in range(CHUNKS):
        core_send_start(0, c)
    loads[0].start()
    loads[1].start()

    requests = n * rows_dev
    slot_row = slots_ref[...]
    sort_map[...] = jnp.where(
        lax.broadcasted_iota(jnp.int32, (requests, requests), 0) == slot_row, 1.0, 0.0
    ).astype(jnp.bfloat16)
    own_slots = lax.broadcasted_iota(jnp.int32, (slots_dev, requests), 0) + me * slots_dev
    own_len = jnp.sum(
        jnp.where(own_slots == slot_row, lens_ref[...].astype(jnp.float32), 0.0), axis=1, keepdims=True
    )
    lens[...] = jnp.broadcast_to(own_len, lens.shape)

    for dist in range(1, half_ring + 1):
        for c in range(CHUNKS):
            for way in range(2):
                cc = c if way == 0 else CHUNKS - 1 - c
                if travels(way, dist, cc):
                    ring_copy(way, dist, cc).wait_recv()
                    if travels(way, dist + 1, cc):
                        ring_send(way, dist + 1, cc)
                    core_send_start(-dist if way == 0 else dist, cc)
        if dist <= 2:
            loads[1 + dist].start()
    for k in range(ring):
        for c in range(CHUNKS):
            core_copy(1 - pool, k, c).wait_recv()

    loads[0].wait()
    loads[1].wait()

    acc_q[...] = jnp.zeros_like(acc_q)
    acc_kv[...] = jnp.zeros_like(acc_kv)
    step = depth // 8

    def project(i, _):
        ks = pl.ds(pl.multiple_of(i * step, step), step)
        acc_q[...] += jnp.dot(x_buf[:, ks], wq[ks, :], preferred_element_type=jnp.float32)
        acc_kv[...] += jnp.dot(x_buf[:, ks], wkv[ks, :], preferred_element_type=jnp.float32)
        return 0

    lax.fori_loop(0, 8, project, 0)
    cols[:, :query_cols] = acc_q[...].astype(jnp.bfloat16)
    cols[:, query_cols:] = acc_kv[...].astype(jnp.bfloat16)
    in_slots = jnp.dot(sort_map[...], cols[...], preferred_element_type=jnp.float32).astype(jnp.bfloat16)
    sendq[...] = in_slots.reshape(sendq.shape)

    def exchange(src, dst, s_sem, r_sem):
        def copy_to(peer, slot):
            return pltpu.make_async_remote_copy(
                src.at[peer], dst.at[slot], s_sem.at[peer], r_sem.at[slot],
                device_id={"pool": peer // ring, "tensor": lax.rem(peer, ring)},
                device_id_type=MESH,
            )

        def start(o, _):
            copy_to(lax.rem(me + o, n), me).start()
            return 0

        def finish(o, _):
            peer = lax.rem(me + o, n)
            copy_to(peer, peer).wait()
            return 0

        lax.fori_loop(1, n, start, 0)
        dst[me] = src[me]
        lax.fori_loop(1, n, finish, 0)

    loads[4].start()
    exchange(sendq, arrived, a_send, a_recv)

    hp = query_cols // HD
    for i in range(n):
        for j in range(hp):
            qbuf[:, i * hp + j, :] = arrived[i, :, j * HD:(j + 1) * HD].astype(jnp.float32)
        kvflat[:, i * kv_cols:(i + 1) * kv_cols] = arrived[i, :, query_cols:].astype(jnp.float32)
    for k in range(kvh):
        kbuf[:, k, :] = kvflat[:, k * HD:(k + 1) * HD]
        vbuf[:, k, :] = kvflat[:, (kvh + k) * HD:(kvh + k + 1) * HD]
    loads[2].wait()
    loads[3].wait()

    row_head = lax.broadcasted_iota(jnp.int32, (heads, kvh * HD), 0) // group
    place = lax.broadcasted_iota(jnp.int32, (heads, length), 1).astype(jnp.float32)
    col_head = lax.broadcasted_iota(jnp.int32, (heads, kvh * HD), 1) // HD
    diagonal = row_head == col_head

    def attend(s):
        q = qbuf[s]
        wide = jnp.where(diagonal, jnp.concatenate([q] * kvh, axis=1), 0.0).astype(jnp.bfloat16)
        scores = lax.dot_general(
            wide, kc[s], (((1,), (1,)), ((), ())), preferred_element_type=jnp.float32
        ) * scale
        scores = jnp.where(place < lens[pl.ds(s, 1), :], scores, -1e30)
        nk = jnp.broadcast_to(kbuf[s][:, None, :], (kvh, group, HD)).reshape(heads, HD)
        nv = jnp.broadcast_to(vbuf[s][:, None, :], (kvh, group, HD)).reshape(heads, HD)
        own = jnp.sum(q * nk, axis=1, keepdims=True) * scale
        top = jnp.maximum(jnp.max(scores, axis=1, keepdims=True), own)
        probs = jnp.exp(scores - top)
        own_prob = jnp.exp(own - top)
        totals = jnp.sum(probs, axis=1, keepdims=True) + own_prob
        full = jnp.dot(probs.astype(jnp.bfloat16), vc[s], preferred_element_type=jnp.float32)
        mine = jnp.concatenate(
            [full[k * group:(k + 1) * group, k * HD:(k + 1) * HD] for k in range(kvh)], axis=0
        )
        mine = mine + own_prob.astype(jnp.bfloat16).astype(jnp.float32) * nv
        obuf[s] = mine / totals

    def attend_some(i, _):
        for j in range(TOGETHER):
            attend(TOGETHER * i + j)
        return 0

    lax.fori_loop(0, slots_dev // TOGETHER, attend_some, 0)

    for i in range(n):
        for j in range(hp):
            sendo[i, :, j * HD:(j + 1) * HD] = obuf[:, i * hp + j, :].astype(jnp.bfloat16)
    exchange(sendo, returned, b_send, b_recv)

    inr[...] = lax.dot_general(
        sort_map[...], returned[...].reshape(requests, query_cols), (((0,), (0,)), ((), ())),
        preferred_element_type=jnp.float32,
    ).astype(jnp.bfloat16)
    loads[4].wait()

    tiles = 2 * SUBS
    tile = depth // tiles
    half_rows = ring * rows_dev

    def pair_copy(c):
        return pltpu.make_async_remote_copy(
            pbuf.at[c, pl.ds(pl.multiple_of((1 - pool) * half_rows, half_rows), half_rows)],
            recvp.at[c], p_send.at[c], p_recv.at[c], device_id=other, device_id_type=MESH,
        )

    def pair_sum(c, t):
        mine = pbuf[c, rows_of(pool, t), :].astype(jnp.float32)
        theirs = recvp[c, pl.ds(pl.multiple_of(t * rows_dev, rows_dev), rows_dev), :]
        return mine + theirs.astype(jnp.float32)

    def hop_copy(src, way, hop, sub):
        return pltpu.make_async_remote_copy(
            src, rbuf.at[way, hop, sub], r_send.at[way, hop, sub], r_recv.at[way, hop, sub],
            device_id=right if way == 0 else left, device_id_type=MESH,
        )

    def set_off(sub):
        for way in range(2):
            c = way * SUBS + sub
            pair_copy(c).wait_recv()
            t = at(-1) if way == 0 else at(1)
            first[way, sub] = pair_sum(c, t).astype(jnp.bfloat16)
            hop_copy(first.at[way, sub], way, 0, sub).start()

    for sub in range(SUBS):
        for way in range(2):
            c = way * SUBS + sub
            pbuf[c] = jnp.dot(
                inr[...], wo[:, c * tile:(c + 1) * tile], preferred_element_type=jnp.float32
            ).astype(jnp.bfloat16)
            pair_copy(c).start()
        if sub >= 1:
            set_off(sub - 1)
    set_off(SUBS - 1)

    def hop_step(hop, _):
        for sub in range(SUBS):
            for way in range(2):
                c = way * SUBS + sub
                here = rbuf.at[way, hop, sub]
                hop_copy(here, way, hop, sub).wait_recv()
                t = at(-2 - hop) if way == 0 else at(2 + hop)
                rbuf[way, hop, sub] = (
                    rbuf[way, hop, sub].astype(jnp.float32) + pair_sum(c, t)
                ).astype(jnp.bfloat16)
                hop_copy(here, way, hop + 1, sub).start()
        return 0

    lax.fori_loop(0, ring - 2, hop_step, 0)
    last = ring - 2
    for sub in range(SUBS):
        for way in range(2):
            c = way * SUBS + sub
            hop_copy(rbuf.at[way, last, sub], way, last, sub).wait_recv()
            out_ref[:, c * tile:(c + 1) * tile] = (
                rbuf[way, last, sub].astype(jnp.float32) + pair_sum(c, t_me)
            ).astype(out_ref.dtype)

    for sub in range(SUBS):
        for way in range(2):
            pair_copy(way * SUBS + sub).wait_send()
            hop_copy(first.at[way, sub], way, 0, sub).wait_send()

    def drain(hop, _):
        for sub in range(SUBS):
            for way in range(2):
                hop_copy(rbuf.at[way, hop - 1, sub], way, hop, sub).wait_send()
        return 0

    lax.fori_loop(1, ring - 1, drain, 0)
    for copy in sent:
        copy.wait_send()


def body(rows, norm_gain, w_query, w_keyval, w_out, key_cache, value_cache, lengths, slot_of):
    pools, ring = lax.axis_size("pool"), lax.axis_size("tensor")
    n = pools * ring
    rows_dev, depth = rows.shape
    slots_dev, length, kv_width = key_cache.shape
    kvh = kv_width // HD
    query_cols, kv_cols = w_query.shape[1], w_keyval.shape[1]
    heads = query_cols * n // HD
    width = query_cols + kv_cols
    requests = rows_dev * n
    half_ring = ring // 2
    tile = depth // (2 * SUBS)
    bf16, f32 = jnp.bfloat16, jnp.float32
    vmem = pl.BlockSpec(memory_space=pltpu.VMEM)
    hbm = pl.BlockSpec(memory_space=pl.ANY)
    dma = pltpu.SemaphoreType.DMA
    return pl.pallas_call(
        functools.partial(kernel, (pools, ring, heads, kvh, rows_dev)),
        out_shape=jax.ShapeDtypeStruct((rows_dev, depth), bf16),
        in_specs=[vmem] * 4 + [hbm] * 5,
        out_specs=vmem,
        scratch_shapes=[
            pltpu.VMEM((requests, depth), bf16),
            pltpu.VMEM(w_query.shape, bf16),
            pltpu.VMEM(w_keyval.shape, bf16),
            pltpu.VMEM(w_out.shape, bf16),
            pltpu.VMEM(key_cache.shape, bf16),
            pltpu.VMEM(value_cache.shape, bf16),
            pltpu.VMEM((requests, query_cols), f32),
            pltpu.VMEM((requests, kv_cols), f32),
            pltpu.VMEM((requests, width), bf16),
            pltpu.VMEM((n, slots_dev, width), bf16),
            pltpu.VMEM((n, slots_dev, width), bf16),
            pltpu.VMEM((slots_dev, heads, HD), f32),
            pltpu.VMEM((slots_dev, kvh, HD), f32),
            pltpu.VMEM((slots_dev, kvh, HD), f32),
            pltpu.VMEM((slots_dev, 2 * kvh * HD), f32),
            pltpu.VMEM((slots_dev, heads, HD), f32),
            pltpu.VMEM((n, slots_dev, query_cols), bf16),
            pltpu.VMEM((n, slots_dev, query_cols), bf16),
            pltpu.VMEM((requests, requests), bf16),
            pltpu.VMEM((slots_dev, length), f32),
            pltpu.VMEM((requests, query_cols), bf16),
            pltpu.VMEM((2 * SUBS, requests, tile), bf16),
            pltpu.VMEM((2 * SUBS, requests // pools, tile), bf16),
            pltpu.VMEM((2, SUBS, rows_dev, tile), bf16),
            pltpu.VMEM((2, ring - 1, SUBS, rows_dev, tile), bf16),
            dma((5,)),
            dma((2, half_ring, CHUNKS)),
            dma((2, half_ring, CHUNKS)),
            dma((ring, CHUNKS)),
            dma((ring, CHUNKS)),
            dma((n,)),
            dma((n,)),
            dma((n,)),
            dma((n,)),
            dma((2 * SUBS,)),
            dma((2 * SUBS,)),
            dma((2, ring - 1, SUBS)),
            dma((2, ring - 1, SUBS)),
        ],
        compiler_params=pltpu.CompilerParams(
            collective_id=0, has_side_effects=True, vmem_limit_bytes=60 * 2**20
        ),
        name="decode_step",
    )(
        slot_of.reshape(1, requests), lengths.reshape(1, requests), rows, norm_gain.reshape(1, depth),
        w_query, w_keyval, w_out, key_cache, value_cache,
    )


def solution(mesh):
    placed = (
        P(("groups", "pool", "tensor"), None),
        P(),
        P(None, ("pool", "tensor")),
        P(None, ("pool", "tensor")),
        P(("pool", "tensor"), None),
        P(("groups", "pool", "tensor"), None, None),
        P(("groups", "pool", "tensor"), None, None),
        P("groups"),
        P("groups"),
    )
    return jax.shard_map(
        body,
        mesh=mesh,
        in_specs=placed,
        out_specs=P(("groups", "pool", "tensor"), None),
        check_vma=False,
    )
```
